512 devices in a mesh: expert: 64 (over x, z), tensor: 8 (over y, core).
Axes of the slice: x: 4, y: 4, z: 16, core: 2. Of those that a mesh axis runs over, the one named last changes fastest.
Arguments:
- first_half: bfloat16 [8192, 2048], P('expert', 'tensor'), may hold values from -6 to 6
- second_half: bfloat16 [8192, 2048], P('expert', 'tensor'), may hold values from -1.5 to 1.5
- first_grad: bfloat16 [8192, 2048], P('expert', 'tensor'), may hold values from -1.5 to 1.5
- second_grad: bfloat16 [8192, 2048], P('expert', 'tensor'), may hold values from -6 to 6
- expert_ids: int32 [8192, 6], P('expert'), may hold values from 0 to 63, as said below
- gate_weights: bfloat16 [8192, 6], P('expert'), may hold values from 0.049804688 to 0.5
- expert_in: bfloat16 [64, 2, 1408, 2048], P('expert', None, 'tensor'), may hold values from -0.125 to 0.125
- expert_out: bfloat16 [64, 1408, 2048], P('expert', 'tensor'), may hold values from -0.15625 to 0.15625
Outputs:
- restored: bfloat16 [8192, 2048], P('expert', 'tensor')
- carried_grad: bfloat16 [8192, 2048], P('expert', 'tensor')
- gate_grad: float32 [8192, 6], P('expert')
- grad_in: bfloat16 [64, 2, 1408, 2048], P('expert', None, 'tensor')
- grad_out: bfloat16 [64, 1408, 2048], P('expert', 'tensor')
The draws below stay inside these ranges and needn't reach their ends.
Inputs may be any that keep to these rules, and one draw needn't show every extreme that they name: `expert_ids`: each token names 6 different experts. In the rows of one index of expert (128 tokens) each expert is named by at least 10 and at most 14 tokens, and one expert is named by exactly 14 tokens of every index of expert.
All inputs are finite; a program needn't handle non-finite values.
Results may differ from the reference program's by a relative error of at most 0.02.
Values may be sent and summed in bfloat16 or wider, within the bound.
A program may use at most 128 MiB of HBM per device.

```python
import math
import jax
import jax.numpy as jnp
from jax import lax

D = 2048
HID = 1408
TOP = 6
TOK_DEV = 128
EXPERTS = 64
TOKENS = 8192
CAP = 14
N_TENSOR = 8


def route_block(key, hot):
    first_key, second_key, third_key = jax.random.split(key, 3)
    order = jax.random.permutation(first_key, EXPERTS).astype(jnp.int32)
    order = jnp.where(order == hot, order[0], order)
    order = order.at[0].set(hot)
    unit = CAP // 7
    share = jax.random.randint(second_key, (EXPERTS // 2,), 0, 2 * unit + 1).astype(jnp.int32)
    share = jnp.where(jnp.arange(EXPERTS // 2) == 0, 0, share)
    removal = jnp.stack([share, 2 * unit - share], axis=1).reshape(EXPERTS)
    loads = CAP - removal
    bounds = jnp.cumsum(loads)
    places = jnp.arange(TOK_DEV * TOP, dtype=jnp.int32)
    ranked = jnp.sum((places[:, None] >= bounds[None, :]).astype(jnp.int32), axis=1)
    sequence = order[ranked]
    layout = sequence.reshape(TOP, TOK_DEV).T
    shuffle = jax.random.permutation(third_key, TOK_DEV)
    return layout[shuffle]


def draw_expert_ids(key, part):
    hot = jax.random.randint(jax.random.fold_in(key, 7), (), 0, EXPERTS).astype(jnp.int32)
    keys = jax.random.split(jax.random.fold_in(key, 11), TOKENS // TOK_DEV)
    blocks = jax.vmap(lambda item: route_block(item, hot))(keys)
    return blocks.reshape(TOKENS, TOP).astype(jnp.int32)


def block_levels(stream_key, dims, pieces, least, high):
    loudness, own = 1.0, jax.random.fold_in(stream_key, 6)
    for axis_at, shards_of in pieces:
        heights = jnp.exp(jax.random.uniform(jax.random.fold_in(own, axis_at), (shards_of,), jnp.float32, least / len(pieces), high / len(pieces)))
        loudness = loudness * jnp.repeat(heights, dims[axis_at] // shards_of).reshape([-1 if axis == axis_at else 1 for axis in range(len(dims))])
    return loudness


def scatter_about(rng, shape, scale, limit, pieces=(), kind=jnp.bfloat16):
    gain = block_levels(rng, shape, pieces, -0.22, 0.18) if pieces else 1.0
    values = jax.random.normal(rng, shape, jnp.float32) * scale * gain
    return jnp.minimum(jnp.maximum(values, -limit), limit).astype(kind)


def setup_inputs(seed: int = 0) -> dict:
    streams_of = jax.random.split(jax.random.key(seed), 9)
    first_half = scatter_about(streams_of[0], (TOKENS, D), 1.0, 6.0, ((0, 64), (1, 8)))
    second_half = scatter_about(streams_of[1], (TOKENS, D), 0.25, 1.5, ((0, 64), (1, 8)))
    first_grad = scatter_about(streams_of[2], (TOKENS, D), 0.25, 1.5, ((0, 64), (1, 8)))
    second_grad = scatter_about(streams_of[3], (TOKENS, D), 1.0, 6.0, ((0, 64), (1, 8)))
    expert_ids = draw_expert_ids(jax.random.fold_in(streams_of[8], 71), 0)
    gate_weights = jnp.clip(jnp.exp(math.log(0.5) - 2.306499 * jax.random.uniform(streams_of[5], (TOKENS, TOP), jnp.float32) ** block_levels(streams_of[5], (TOKENS, TOP), ((0, 64),), -0.2, 0.2)), 0.049804688, 0.5).astype(jnp.bfloat16)
    expert_in = scatter_about(streams_of[6], (EXPERTS, 2, HID, D), D ** -0.5, 0.125, ((0, 64), (2, 8)))
    expert_out = scatter_about(streams_of[7], (EXPERTS, HID, D), HID ** -0.5, 0.15625, ((0, 64), (1, 8)))
    return {"first_half": first_half, "second_half": second_half, "first_grad": first_grad, "second_grad": second_grad, "expert_ids": expert_ids, "gate_weights": gate_weights, "expert_in": expert_in, "expert_out": expert_out}


def settle(values):
    return lax.optimization_barrier(values.astype(jnp.bfloat16)).astype(jnp.float32)


def reference(first_half, second_half, first_grad, second_grad, expert_ids, gate_weights, expert_in, expert_out):
    blocks = TOKENS // TOK_DEV
    routes = expert_ids.reshape(blocks, TOK_DEV * TOP)
    onehot = (routes[:, :, None] == jnp.arange(EXPERTS, dtype=jnp.int32)[None, None, :]).astype(jnp.int32)
    before = jnp.cumsum(onehot, axis=1) - onehot
    slot_index = jnp.sum(before * onehot, axis=2).reshape(-1).astype(jnp.int32)
    flat = expert_ids.reshape(-1).astype(jnp.int32)
    count = TOKENS * TOP
    route_ids = jnp.arange(count, dtype=jnp.int32)
    source = route_ids // (TOK_DEV * TOP)
    position = flat * (blocks * CAP) + source * CAP + slot_index
    slot_route = jnp.full((EXPERTS * blocks * CAP,), count, jnp.int32).at[position].set(route_ids)
    slot_route = slot_route.reshape(EXPERTS, blocks * CAP)
    route_token = jnp.concatenate([route_ids // TOP, jnp.full((1,), TOKENS, jnp.int32)])
    gate_pad = jnp.concatenate([gate_weights.reshape(-1), jnp.zeros((1,), jnp.bfloat16)])
    first_pad = jnp.concatenate([first_half, jnp.zeros((1, D), jnp.bfloat16)], axis=0)
    cot_pad = jnp.concatenate([second_grad, jnp.zeros((1, D), jnp.bfloat16)], axis=0)
    width = HID // N_TENSOR

    def one_expert(carry, inputs):
        out_acc, dx_acc, gate_acc = carry
        picked, weights_in, weights_out = inputs
        token_rows = route_token[picked]
        slot_rows = first_pad[token_rows]
        slot_cots = cot_pad[token_rows]
        slot_gates = gate_pad[picked].astype(jnp.float32)
        scaled = (slot_gates[:, None] * slot_cots.astype(jnp.float32)).astype(jnp.bfloat16)
        out_sum = jnp.zeros((slot_rows.shape[0], D), jnp.float32)
        dx_sum = jnp.zeros((slot_rows.shape[0], D), jnp.float32)
        gate_sum = jnp.zeros((slot_rows.shape[0],), jnp.float32)
        grads_in = []
        grads_out = []
        for group in range(N_TENSOR):
            w_gate = weights_in[0][group * width:(group + 1) * width, :]
            w_up = weights_in[1][group * width:(group + 1) * width, :]
            w_down = weights_out[group * width:(group + 1) * width, :]
            gate_pre = jnp.dot(slot_rows, w_gate.T, preferred_element_type=jnp.float32)
            up_pre = jnp.dot(slot_rows, w_up.T, preferred_element_type=jnp.float32)
            sigma = jax.nn.sigmoid(gate_pre)
            active = gate_pre * sigma
            hidden = (active * up_pre).astype(jnp.bfloat16)
            part_out = jnp.dot(hidden, w_down, preferred_element_type=jnp.float32)
            out_sum = out_sum + settle(part_out)
            gate_sum = gate_sum + settle(jnp.sum(slot_cots.astype(jnp.float32) * part_out, axis=1))
            hidden_grad = jnp.dot(scaled, w_down.T, preferred_element_type=jnp.float32)
            gate_pre_grad = (hidden_grad * up_pre * sigma * (1.0 + gate_pre * (1.0 - sigma))).astype(jnp.bfloat16)
            up_grad = (hidden_grad * active).astype(jnp.bfloat16)
            input_piece = jnp.dot(gate_pre_grad, w_gate, preferred_element_type=jnp.float32) + jnp.dot(up_grad, w_up, preferred_element_type=jnp.float32)
            dx_sum = dx_sum + settle(input_piece)
            grads_in.append(jnp.stack([jnp.dot(gate_pre_grad.T, slot_rows, preferred_element_type=jnp.float32), jnp.dot(up_grad.T, slot_rows, preferred_element_type=jnp.float32)]).astype(jnp.bfloat16))
            grads_out.append(jnp.dot(hidden.T, scaled, preferred_element_type=jnp.float32).astype(jnp.bfloat16))
        out_acc = out_acc.at[token_rows].add(slot_gates[:, None] * out_sum)
        dx_acc = dx_acc.at[token_rows].add(dx_sum)
        gate_acc = gate_acc.at[picked].add(gate_sum)
        return (out_acc, dx_acc, gate_acc), (jnp.concatenate(grads_in, axis=1), jnp.concatenate(grads_out, axis=0))

    start = (jnp.zeros((TOKENS + 1, D), jnp.float32), jnp.zeros((TOKENS + 1, D), jnp.float32), jnp.zeros((count + 1,), jnp.float32))
    (out_acc, dx_acc, gate_acc), (grad_in, grad_out) = lax.scan(one_expert, start, (slot_route, expert_in, expert_out))
    restored = (second_half.astype(jnp.float32) - out_acc[:TOKENS]).astype(jnp.bfloat16)
    carried_grad = (first_grad.astype(jnp.float32) + dx_acc[:TOKENS]).astype(jnp.bfloat16)
    gate_grad = gate_acc[:count].reshape(TOKENS, TOP)
    return restored, carried_grad, gate_grad, grad_in, grad_out
```

```python
import jax
import jax.numpy as jnp
from jax import lax
from jax.sharding import PartitionSpec as P

F32, BF16 = jnp.float32, jnp.bfloat16


def body(
    first_half,
    second_half,
    first_grad,
    second_grad,
    expert_ids,
    gate_weights,
    expert_in,
    expert_out,
):
    tokens, picks = expert_ids.shape
    experts = lax.axis_size("expert")
    cap = tokens * picks * 7 // (6 * experts)
    columns = first_half.shape[1]
    hits = expert_ids[:, :, None] == jnp.arange(experts, dtype=jnp.int32)
    member = jnp.any(hits, axis=1)
    gate = jnp.sum(jnp.where(hits, gate_weights.astype(F32)[:, :, None], 0.0), axis=1)
    below = (jnp.arange(tokens)[:, None] > jnp.arange(tokens)[None, :]).astype(BF16)
    rank = jnp.dot(below, member.astype(BF16), preferred_element_type=F32)
    slot = jnp.arange(cap, dtype=F32)
    chosen = member.T[:, None, :] & (rank.T[:, None, :] == slot[None, :, None])
    pick = chosen.astype(BF16).reshape(experts * cap, tokens)
    weigh = jnp.where(chosen, gate.T[:, None, :], 0.0).astype(BF16)
    weigh = weigh.reshape(experts * cap, tokens)

    def over(values):
        shaped = values.reshape(experts, cap, columns)
        moved = lax.all_to_all(shaped, "expert", split_axis=0, concat_axis=0, tiled=True)
        return moved.reshape(experts * cap, columns)

    rows = jnp.dot(pick, first_half, preferred_element_type=F32).astype(BF16)
    scaled_mine = jnp.dot(weigh, second_grad, preferred_element_type=F32).astype(BF16)
    rows_all = lax.all_gather(over(rows), "tensor", axis=1, tiled=True)
    scaled = lax.all_gather(over(scaled_mine), "tensor", axis=1, tiled=True)
    w_gate, w_up, w_down = expert_in[0, 0], expert_in[0, 1], expert_out[0]

    def mm(spec, a, b):
        return jnp.einsum(spec, a, b, preferred_element_type=F32)

    gate_pre = mm("rd,hd->rh", rows_all, w_gate)
    up_pre = mm("rd,hd->rh", rows_all, w_up)
    sigma = jax.nn.sigmoid(gate_pre)
    active = gate_pre * sigma
    hidden = (active * up_pre).astype(BF16)
    part_out = mm("rh,hd->rd", hidden, w_down).astype(BF16)
    hidden_grad = mm("rd,hd->rh", scaled, w_down)
    gate_pre_grad = (hidden_grad * up_pre * sigma * (1.0 + gate_pre * (1.0 - sigma))).astype(BF16)
    up_grad = (hidden_grad * active).astype(BF16)
    input_piece = (mm("rh,hd->rd", gate_pre_grad, w_gate) + mm("rh,hd->rd", up_grad, w_up)).astype(BF16)
    out_mine = lax.psum_scatter(part_out, "tensor", scatter_dimension=1, tiled=True)
    input_mine = lax.psum_scatter(input_piece, "tensor", scatter_dimension=1, tiled=True)
    grad_gate = mm("rh,rd->hd", gate_pre_grad, rows_all).astype(BF16)
    grad_up = mm("rh,rd->hd", up_grad, rows_all).astype(BF16)
    grad_out = mm("rh,rd->hd", hidden, scaled).astype(BF16)
    back_out, back_input = over(out_mine), over(input_mine)
    branch = mm("st,sd->td", weigh, back_out)
    branch_grad = mm("st,sd->td", pick, back_input)
    dots = jnp.sum(scaled_mine.astype(F32) * back_out.astype(F32), axis=1)
    table = jnp.sum(jnp.where(chosen, dots.reshape(experts, cap, 1), 0.0), axis=1).T
    parts = jnp.sum(jnp.where(hits, table[:, None, :], 0.0), axis=2) / gate_weights.astype(F32)
    gate_grad = lax.psum(parts, "tensor")
    restored = (second_half.astype(F32) - branch).astype(BF16)
    carried_grad = (first_grad.astype(F32) + branch_grad).astype(BF16)
    return (restored, carried_grad, gate_grad, jnp.stack([grad_gate, grad_up])[None], grad_out[None])


def solution(mesh):
    tokens = P("expert", "tensor")
    routes = P("expert", None)
    weights = (P("expert", None, "tensor", None), P("expert", "tensor", None))
    return jax.shard_map(
        body,
        mesh=mesh,
        in_specs=(tokens, tokens, tokens, tokens, routes, routes, *weights),
        out_specs=(tokens, tokens, routes, *weights),
        check_vma=False,
    )
```

```python
import jax
import jax.numpy as jnp
from jax import lax
from jax.experimental import pallas as pl
from jax.experimental.pallas import tpu as pltpu
from jax.sharding import PartitionSpec as P

F32, BF16 = jnp.float32, jnp.bfloat16
X, Y, Z = 4, 4, 16
T, C, H, D, CAP, K = 128, 256, 176, 2048, 14, 8
M = 8 * CAP
G = 4 * M
RIGHT = (0, 1, 2, 3, 4, 8, 9, 10, 11)
LEFT = (0, 5, 6, 7, 12, 13, 14, 15, 11)
NT = (((1,), (1,)), ((), ()))
TN = (((0,), (0,)), ((), ()))
MESH = pl.DeviceIdType.MESH


def mm(a, b, dims=(((1,), (0,)), ((), ()))):
    return lax.dot_general(a, b, dims, preferred_element_type=F32)


def kernel(
    fh, sg, sh, fg, meta, win, wdn,
    res, car, gat, gin, gout,
    rb, cb, pu, pw, xs, ra, w, pre, hs, ht, po, pb, rl, fr, fb, ret, con, gt, zr, gb, gs,
    zsem, xsem, ysem, rsem, bsem, qsem, gsem, wsem, osem,
):
    e, t = lax.axis_index("expert"), lax.axis_index("tensor")
    x, z, y, c = e // Z, e % Z, t // 2, t % 2
    right, left = (x * Z + (z + 1) % Z, t), (x * Z + (z + Z - 1) % Z, t)
    up, down = (e, ((y + 1) % Y) * 2 + c), (e, ((y + Y - 1) % Y) * 2 + c)
    sib = (e, y * 2 + 1 - c)
    ahead = [(((x + d) % X) * Z + z, t) for d in range(X)]
    behind = [(((x + X - d) % X) * Z + z, t) for d in range(X)]
    peers = [(e, (t + r) % 8) for r in range(8)]

    loads = []
    for j in range(8):
        col = pl.multiple_of((((y + Y - j % 4) % Y) * 2 + (c + j // 4) % 2) * C, C)
        for k in range(3):
            src = win.at[k, :, pl.ds(col, C)] if k < 2 else wdn.at[:, pl.ds(col, C)]
            loads.append(pltpu.make_async_copy(src, w.at[k, j], wsem.at[k, j]))
            loads[-1].start()
    rb[0, 0:T, :] = fh[...]
    rb[0, T : T + 16, :] = meta[...]
    cb[0] = sg[...]

    barrier = pltpu.get_barrier_semaphore()
    for dev in [right, left, *ahead[1:], *peers[1:]]:
        pl.semaphore_signal(barrier, inc=1, device_id=dev, device_id_type=MESH)
    pl.semaphore_wait(barrier, 12)

    sent = []

    def send(src, dst, sems, at, dev):
        copy = pltpu.make_async_remote_copy(
            src_ref=src,
            dst_ref=dst,
            send_sem=sems.at[(0, *at)],
            recv_sem=sems.at[(1, *at)],
            device_id=dev,
            device_id_type=MESH,
        )
        copy.start()
        sent.append(copy)
        return copy

    zcopy = {}
    zlast = {(0, 0): 8, (0, 1): 7, (1, 0): 7, (1, 1): 8}

    def zstep(s):
        for a in range(2):
            buf = (rb, cb)[a]
            for d in range(2):
                place = (RIGHT, LEFT)[d]
                if s > 1 and s - 1 <= zlast[a, d]:
                    zcopy[a, d, s - 1].wait_recv()
                if s <= zlast[a, d]:
                    zcopy[a, d, s] = send(
                        buf.at[place[s - 1]], buf.at[place[s]], zsem, (a, place[s]), (right, left)[d]
                    )

    before = lax.broadcasted_iota(jnp.int32, (T, T), 0) < lax.broadcasted_iota(jnp.int32, (T, T), 1)
    before = jnp.where(before, 1.0, 0.0).astype(BF16)

    def experts(d):
        return (((x + d) % X) * Z + z).astype(F32)

    def slots(g):
        ids = rb[8 * g : 8 * g + 8, T : T + 16, 0:128].astype(F32)
        gates = rb[8 * g : 8 * g + 8, T : T + 16, 128:256].astype(F32)
        member, weight = [], []
        for d in range(X):
            hit = ids == experts(d)
            member.append(jnp.sum(jnp.where(hit, 1.0, 0.0), axis=1))
            weight.append(jnp.sum(jnp.where(hit, gates, 0.0), axis=1))
        member, weight = jnp.concatenate(member, axis=0), jnp.concatenate(weight, axis=0)
        rank = mm(member.astype(BF16), before)
        source = lax.broadcasted_iota(jnp.int32, (32, T), 0) % 8
        place = jnp.where(member > 0.5, rank + (CAP * source).astype(F32), -1.0)
        row = lax.broadcasted_iota(jnp.int32, (M, T), 0).astype(F32)
        for d in range(X):
            for i in range(8):
                n = 8 * d + i
                here = row == place[n : n + 1, :]
                pu[g, M * d : M * d + M, T * i : T * i + T] = jnp.where(here, 1.0, 0.0).astype(BF16)
                pw[g, M * d : M * d + M, T * i : T * i + T] = jnp.where(
                    here, jnp.broadcast_to(weight[n : n + 1, :], (M, T)), 0.0
                ).astype(BF16)

    xcopy = {}

    def xsend(a, g):
        if a == 0:
            chosen = mm(pu[g], rb[8 * g : 8 * g + 8, 0:T, :].reshape(8 * T, C))
        else:
            chosen = mm(pw[g], cb[8 * g : 8 * g + 8].reshape(8 * T, C))
        chosen = chosen.astype(BF16).reshape(X, M, C)
        xs[a, g] = chosen
        ra[a, 0, 4 * g] = chosen[0]
        for d in range(1, X):
            xcopy[a, g, d] = send(
                xs.at[a, g, d], ra.at[a, 0, 4 * g + d], xsem, (a, g, d - 1), ahead[d]
            )

    ycopy = {}

    def ysend(a, g):
        for d in range(1, X):
            xcopy[a, g, d].wait_recv()
        own = ra.at[a, 0, pl.ds(4 * g, 4)]
        for n, (j, dev) in enumerate(((1, up), (3, down), (4, sib))):
            ycopy[a, g, n] = send(own, ra.at[a, j, pl.ds(4 * g, 4)], ysem, (a, g, n), dev)

    def yforward(a, g):
        for n, j, at, dev in ((0, 1, 0, up), (1, 3, 2, down)):
            ycopy[a, g, n].wait_recv()
            half = pl.ds(4 * g + at, 2)
            ycopy[a, g, 3 + n] = send(ra.at[a, j, half], ra.at[a, 2, half], ysem, (a, g, 3 + n), dev)
            whole = pl.ds(4 * g, 4)
            ycopy[a, g, 4 + j] = send(
                ra.at[a, j, whole], ra.at[a, 4 + j, whole], ysem, (a, g, 4 + j), sib
            )

    def yfinish(a, g):
        ycopy[a, g, 3].wait_recv()
        ycopy[a, g, 4].wait_recv()
        whole = pl.ds(4 * g, 4)
        ycopy[a, g, 6] = send(ra.at[a, 2, whole], ra.at[a, 6, whole], ysem, (a, g, 6), sib)

    def yall(a, g):
        for n in (2, 5, 6, 7):
            ycopy[a, g, n].wait_recv()

    def block(ref, a, j, g):
        return ref[a, j, 4 * g : 4 * g + 4].reshape(G, C)

    def first(g):
        for k, a in ((0, 0), (1, 0), (2, 1)):
            for half in range(2):
                js = range(4 * half, 4 * half + 4)
                rows = jnp.concatenate([block(ra, a, j, g) for j in js], axis=1)
                part = mm(rows, jnp.concatenate([w[k, j] for j in js], axis=1), NT)
                pre[k] = part if half == 0 else pre[k] + part

        def gates(i, _):
            at = pl.ds(pl.multiple_of(i * M, 8), M)
            gate_pre, up_pre, hidden_grad = pre[0, at, :], pre[1, at, :], pre[2, at, :]
            sigma = jax.nn.sigmoid(gate_pre)
            active = gate_pre * sigma
            slope = hidden_grad * up_pre * sigma * (1.0 + gate_pre * (1.0 - sigma))
            for k, value in enumerate((active * up_pre, slope, hidden_grad * active)):
                hs[k, 4 * g + i, :, 0:H] = value.astype(BF16)
            return 0

        lax.fori_loop(0, 4, gates, 0)

    rcopy = {}

    def pieces(a, g):
        def one(j, _):
            if a == 0:
                part = mm(hs[0, 4 * g : 4 * g + 4].reshape(G, C)[:, 0:H], w[2, j])
            else:
                part = mm(hs[1, 4 * g : 4 * g + 4].reshape(G, C)[:, 0:H], w[0, j])
                part += mm(hs[2, 4 * g : 4 * g + 4].reshape(G, C)[:, 0:H], w[1, j])
            po[a, g, j] = part.astype(BF16).reshape(X, M, C)
            return 0

        lax.fori_loop(0, 8, one, 0)
        for n in (2, 1, 3, 0):
            rcopy[a, g, n] = send(po.at[a, g, 4 + n], pb.at[a, g, n], rsem, (a, g, n), sib)

    def total(a, g, n):
        rcopy[a, g, n].wait_recv()

        def one(i, _):
            po[a, g, n, i] = (po[a, g, n, i].astype(F32) + pb[a, g, n, i].astype(F32)).astype(BF16)
            return 0

        lax.fori_loop(0, 4, one, 0)

    def reduce_far(a, g):
        total(a, g, 2)
        for n, dev in ((0, down), (1, up)):
            rcopy[a, g, 4 + n] = send(
                po.at[a, g, 2, pl.ds(2 * n, 2)], rl.at[a, g, n], rsem, (a, g, 4 + n), dev
            )

    def reduce_near(a, g):
        for n, j, dev in ((0, 1, down), (1, 3, up)):
            total(a, g, j)
            rcopy[a, g, 4 + n].wait_recv()
            for i in range(2):
                po[a, g, j, 2 * n + i] = (
                    po[a, g, j, 2 * n + i].astype(F32) + rl[a, g, n, i].astype(F32)
                ).astype(BF16)
            rcopy[a, g, 6 + n] = send(po.at[a, g, j], fr.at[a, g, n], rsem, (a, g, 6 + n), dev)

    bcopy = {}

    def give_back(a, g):
        for n in (0, 6, 7):
            rcopy[a, g, n].wait_recv()

        def one(i, _):
            fb[a, g, i] = (
                po[a, g, 0, i].astype(F32)
                + pb[a, g, 0, i].astype(F32)
                + fr[a, g, 0, i].astype(F32)
                + fr[a, g, 1, i].astype(F32)
            ).astype(BF16)
            return 0

        lax.fori_loop(0, 4, one, 0)
        ret[a, g, 0] = fb[a, g, 0]
        for d in range(1, X):
            bcopy[a, g, d] = send(fb.at[a, g, d], ret.at[a, g, d], bsem, (a, g, d - 1), behind[d])

    def combine(a, g):
        for d in range(1, X):
            bcopy[a, g, d].wait_recv()
        rows = ret[a, g].reshape(G, C)
        table = (pw, pu)[a]
        for i in range(8):
            con[a, 8 * g + i] = mm(table[g, :, T * i : T * i + T], rows, TN)
        if a == 0:
            dots = jnp.sum(
                xs[1, g].reshape(G, C).astype(F32) * rows.astype(F32), axis=1, keepdims=True
            )
            for i in range(8):
                spread = pu[g, :, T * i : T * i + T].astype(F32) * dots
                ids = rb[8 * g + i, T : T + 16, 0:128].astype(F32)
                gates = rb[8 * g + i, T : T + 16, 128:256].astype(F32)
                parts = jnp.zeros((16, T), F32)
                for d in range(X):
                    line = jnp.sum(spread[M * d : M * d + M], axis=0, keepdims=True)
                    parts += jnp.where(ids == experts(d), line, 0.0)
                gt[8 * g + i] = parts / gates

    qcopy = {}
    qfirst = {(0, 0): 7, (0, 1): 8, (1, 0): 8, (1, 1): 7}

    def qsend(a, d, s):
        rows = pl.ds(0, T + 16 if a == 0 else T)
        qcopy[a, d, s] = send(
            zr.at[a, d, s, rows], zr.at[a, d, s - 1, rows], qsem, (a, d, s - 1), (right, left)[d]
        )

    def qstart(a):
        for d in range(2):
            s = qfirst[a, d]
            place = (LEFT, RIGHT)[d][s]
            zr[a, d, s, 0:T] = con[a, place].astype(BF16)
            if a == 0:
                zr[a, d, s, T : T + 16, 0:128] = gt[place].astype(BF16)
                zr[a, d, s, T : T + 16, 128:256] = jnp.zeros((16, 128), BF16)
            qsend(a, d, s)

    def qstep(a, back):
        for d in range(2):
            s = qfirst[a, d] - back
            if s < 0:
                continue
            qcopy[a, d, s + 1].wait_recv()
            if s == 0:
                continue
            place = (LEFT, RIGHT)[d][s]
            zr[a, d, s, 0:T] = (zr[a, d, s, 0:T].astype(F32) + con[a, place]).astype(BF16)
            if a == 0:
                zr[a, d, s, T : T + 16, 0:128] = (
                    zr[a, d, s, T : T + 16, 0:128].astype(F32) + gt[place]
                ).astype(BF16)
            qsend(a, d, s)

    def weight_grads():
        for k in range(3):
            ht[k] = jnp.transpose(hs[k].reshape(2 * G, C))

        def one(j, _):
            for k, n, a in ((0, 1, 0), (1, 2, 0), (2, 0, 1)):
                gs[k, j] = mm(ht[n, 0:H, :], ra[a, j].reshape(2 * G, C)).astype(BF16)
            return 0

        lax.fori_loop(0, 8, one, 0)
        for j in range(8):
            col = pl.multiple_of((((y + Y - j % 4) % Y) * 2 + (c + j // 4) % 2) * C, C)
            for k in range(3):
                dst = gin.at[k, :, pl.ds(col, C)] if k < 2 else gout.at[:, pl.ds(col, C)]
                sent_local.append(pltpu.make_async_copy(gs.at[k, j], dst, osem.at[k, j]))
                sent_local[-1].start()

    sent_local = []

    zstep(1)
    hs[:, :, :, 128:256] = jnp.zeros((3, 8, M, 128), BF16)
    for s in (2, 3, 4, 5):
        zstep(s)
    slots(0)
    xsend(0, 0)
    xsend(1, 0)
    zstep(6)
    ysend(0, 0)
    ysend(1, 0)
    zstep(7)
    yforward(0, 0)
    zstep(8)
    yforward(1, 0)
    for load in loads:
        load.wait()
    zstep(9)
    slots(1)
    xsend(0, 1)
    xsend(1, 1)
    yfinish(0, 0)
    ysend(0, 1)
    yfinish(1, 0)
    ysend(1, 1)
    yall(0, 0)
    yall(1, 0)
    first(0)
    yforward(0, 1)
    pieces(0, 0)
    yforward(1, 1)
    yfinish(0, 1)
    pieces(1, 0)
    reduce_far(0, 0)
    yfinish(1, 1)
    yall(0, 1)
    yall(1, 1)
    first(1)
    pieces(0, 1)
    reduce_near(0, 0)
    reduce_far(0, 1)
    reduce_far(1, 0)
    pieces(1, 1)
    reduce_near(0, 1)
    give_back(0, 0)
    reduce_near(1, 0)
    reduce_far(1, 1)
    give_back(0, 1)
    combine(0, 0)
    give_back(1, 0)
    reduce_near(1, 1)
    combine(0, 1)
    qstart(0)
    weight_grads()
    qstep(0, 1)
    give_back(1, 1)
    combine(1, 0)
    qstep(0, 2)
    combine(1, 1)
    qstart(1)
    for back in range(3, 9):
        qstep(0, back)
        qstep(1, back - 2)

    here = gt[0] + zr[0, 0, 0, T : T + 16, 0:128].astype(F32) + zr[0, 1, 0, T : T + 16, 0:128].astype(F32)
    gb[0] = here[0:8]
    gcopy = [send(gb.at[0], gb.at[r], gsem, (r - 1,), peers[r]) for r in range(1, 8)]
    branch = con[0, 0] + zr[0, 0, 0, 0:T].astype(F32) + zr[0, 1, 0, 0:T].astype(F32)
    res[...] = (sh[...].astype(F32) - branch).astype(BF16)
    for copy in gcopy:
        copy.wait_recv()
    gat[...] = sum(gb[r] for r in range(8))
    qstep(1, 7)
    qstep(1, 8)
    branch = con[1, 0] + zr[1, 0, 0, 0:T].astype(F32) + zr[1, 1, 0, 0:T].astype(F32)
    car[...] = (fg[...].astype(F32) + branch).astype(BF16)
    for copy in sent:
        copy.wait_send()
    for copy in sent_local:
        copy.wait()


def body(first_half, second_half, first_grad, second_grad, expert_ids, gate_weights, expert_in, expert_out):
    ids = jnp.pad(expert_ids.T.astype(BF16), ((0, 10), (0, 0)), constant_values=-1)
    gates = jnp.pad(gate_weights.T, ((0, 10), (0, 0)), constant_values=1)
    meta = jnp.concatenate([ids, gates], axis=1)
    vmem, hbm = pl.BlockSpec(memory_space=pltpu.VMEM), pl.BlockSpec(memory_space=pl.ANY)
    dma = pltpu.SemaphoreType.DMA
    shape = jax.ShapeDtypeStruct
    res, car, gat, gin, gout = pl.pallas_call(
        kernel,
        out_shape=(
            shape((T, C), BF16),
            shape((T, C), BF16),
            shape((8, T), F32),
            shape((2, H, D), BF16),
            shape((H, D), BF16),
        ),
        in_specs=[vmem] * 5 + [hbm] * 2,
        out_specs=(vmem, vmem, vmem, hbm, hbm),
        scratch_shapes=[
            pltpu.VMEM((16, T + 16, C), BF16),
            pltpu.VMEM((16, T, C), BF16),
            pltpu.VMEM((2, G, 8 * T), BF16),
            pltpu.VMEM((2, G, 8 * T), BF16),
            pltpu.VMEM((2, 2, X, M, C), BF16),
            pltpu.VMEM((2, 8, 8, M, C), BF16),
            pltpu.VMEM((3, 8, H, C), BF16),
            pltpu.VMEM((3, G, H), F32),
            pltpu.VMEM((3, 8, M, C), BF16),
            pltpu.VMEM((3, C, 2 * G), BF16),
            pltpu.VMEM((2, 2, 8, X, M, C), BF16),
            pltpu.VMEM((2, 2, 4, X, M, C), BF16),
            pltpu.VMEM((2, 2, 2, 2, M, C), BF16),
            pltpu.VMEM((2, 2, 2, X, M, C), BF16),
            pltpu.VMEM((2, 2, X, M, C), BF16),
            pltpu.VMEM((2, 2, X, M, C), BF16),
            pltpu.VMEM((2, 16, T, C), F32),
            pltpu.VMEM((16, 16, T), F32),
            pltpu.VMEM((2, 2, 9, T + 16, C), BF16),
            pltpu.VMEM((8, 8, T), F32),
            pltpu.VMEM((3, 8, H, C), BF16),
            dma((2, 2, 16)),
            dma((2, 2, 2, 3)),
            dma((2, 2, 2, 8)),
            dma((2, 2, 2, 8)),
            dma((2, 2, 2, 3)),
            dma((2, 2, 2, 8)),
            dma((2, 7)),
            dma((3, 8)),
            dma((3, 8)),
        ],
        compiler_params=pltpu.CompilerParams(
            collective_id=0, has_side_effects=True, vmem_limit_bytes=58 * 2**20
        ),
    )(first_half, second_grad, second_half, first_grad, meta, expert_in[0], expert_out[0])
    return res, car, gat[0:6].T, gin[None], gout[None]


def solution(mesh):
    tokens = P("expert", "tensor")
    routes = P("expert", None)
    weights = (P("expert", None, "tensor", None), P("expert", "tensor", None))
    return jax.shard_map(
        body,
        mesh=mesh,
        in_specs=(tokens, tokens, tokens, tokens, routes, routes, *weights),
        out_specs=(tokens, tokens, routes, *weights),
        check_vma=False,
    )
```

```python
import jax
import jax.numpy as jnp
from jax import lax
from jax.experimental import pallas as pl
from jax.experimental.pallas import tpu as pltpu
from jax.sharding import PartitionSpec as P

F32, BF16 = jnp.float32, jnp.bfloat16
X, Y, Z = 4, 4, 16
T, C, H, D, CAP, K = 128, 256, 176, 2048, 14, 8
M = 8 * CAP
G = 4 * M
RIGHT = (0, 1, 2, 3, 4, 8, 9, 10, 11)
LEFT = (0, 5, 6, 7, 12, 13, 14, 15, 11)
NT = (((1,), (1,)), ((), ()))
TN = (((0,), (0,)), ((), ()))
MESH = pl.DeviceIdType.MESH


def mm(a, b, dims=(((1,), (0,)), ((), ()))):
    return lax.dot_general(a, b, dims, preferred_element_type=F32)


def kernel(
    fh, sg, sh, fg, ids, gates, win, wdn,
    res, car, gat, gin, gout,
    rb, cb, pu, pw, xs, ra, w, pre, hs, ht, po, pb, rl, fr, fb, ret, con, gt, zr, gb, gs,
    zsem, xsem, ysem, rsem, bsem, qsem, gsem, wsem, osem,
):
    e, t = lax.axis_index("expert"), lax.axis_index("tensor")
    x, z, y, c = e // Z, e % Z, t // 2, t % 2
    right, left = (x * Z + (z + 1) % Z, t), (x * Z + (z + Z - 1) % Z, t)
    up, down = (e, ((y + 1) % Y) * 2 + c), (e, ((y + Y - 1) % Y) * 2 + c)
    sib = (e, y * 2 + 1 - c)
    ahead = [(((x + d) % X) * Z + z, t) for d in range(X)]
    behind = [(((x + X - d) % X) * Z + z, t) for d in range(X)]
    peers = [(e, (t + r) % 8) for r in range(8)]

    loads = []
    for j in range(8):
        col = pl.multiple_of((((y + Y - j % 4) % Y) * 2 + (c + j // 4) % 2) * C, C)
        for k in range(3):
            src = win.at[k, :, pl.ds(col, C)] if k < 2 else wdn.at[:, pl.ds(col, C)]
            loads.append(pltpu.make_async_copy(src, w.at[k, j], wsem.at[k, j]))
            loads[-1].start()
    rb[0, 0:T, :] = fh[...]
    blank = jnp.ones((10, T), F32)
    names = jnp.concatenate([ids[...].astype(F32), -blank], axis=0)
    rb[0, T : T + 16, 0:128] = names.astype(BF16)
    rb[0, T : T + 16, 128:256] = jnp.concatenate([gates[...].astype(F32), blank], axis=0).astype(BF16)
    cb[0] = sg[...]

    barrier = pltpu.get_barrier_semaphore()
    for dev in [right, left, *ahead[1:], *peers[1:]]:
        pl.semaphore_signal(barrier, inc=1, device_id=dev, device_id_type=MESH)
    pl.semaphore_wait(barrier, 12)

    sent = []

    def send(src, dst, sems, at, dev):
        copy = pltpu.make_async_remote_copy(
            src_ref=src,
            dst_ref=dst,
            send_sem=sems.at[(0, *at)],
            recv_sem=sems.at[(1, *at)],
            device_id=dev,
            device_id_type=MESH,
        )
        copy.start()
        sent.append(copy)
        return copy

    zcopy = {}
    zlast = {(0, 0): 8, (0, 1): 7, (1, 0): 7, (1, 1): 8}

    def zstep(s):
        for a in range(2):
            buf = (rb, cb)[a]
            for d in range(2):
                place = (RIGHT, LEFT)[d]
                if s > 1 and s - 1 <= zlast[a, d]:
                    zcopy[a, d, s - 1].wait_recv()
                if s <= zlast[a, d]:
                    zcopy[a, d, s] = send(
                        buf.at[place[s - 1]], buf.at[place[s]], zsem, (a, place[s]), (right, left)[d]
                    )

    before = lax.broadcasted_iota(jnp.int32, (T, T), 0) < lax.broadcasted_iota(jnp.int32, (T, T), 1)
    before = jnp.where(before, 1.0, 0.0).astype(BF16)

    def experts(d):
        return (((x + d) % X) * Z + z).astype(F32)

    def slots(g):
        ids = rb[8 * g : 8 * g + 8, T : T + 16, 0:128].astype(F32)
        gates = rb[8 * g : 8 * g + 8, T : T + 16, 128:256].astype(F32)
        member, weight = [], []
        for d in range(X):
            hit = ids == experts(d)
            member.append(jnp.sum(jnp.where(hit, 1.0, 0.0), axis=1))
            weight.append(jnp.sum(jnp.where(hit, gates, 0.0), axis=1))
        member, weight = jnp.concatenate(member, axis=0), jnp.concatenate(weight, axis=0)
        rank = mm(member.astype(BF16), before)
        source = lax.broadcasted_iota(jnp.int32, (32, T), 0) % 8
        place = jnp.where(member > 0.5, rank + (CAP * source).astype(F32), -1.0)
        row = lax.broadcasted_iota(jnp.int32, (M, T), 0).astype(F32)
        for d in range(X):
            for i in range(8):
                n = 8 * d + i
                here = row == place[n : n + 1, :]
                pu[g, M * d : M * d + M, T * i : T * i + T] = jnp.where(here, 1.0, 0.0).astype(BF16)
                pw[g, M * d : M * d + M, T * i : T * i + T] = jnp.where(
                    here, jnp.broadcast_to(weight[n : n + 1, :], (M, T)), 0.0
                ).astype(BF16)

    xcopy = {}

    def xsend(a, g):
        if a == 0:
            chosen = mm(pu[g], rb[8 * g : 8 * g + 8, 0:T, :].reshape(8 * T, C))
        else:
            chosen = mm(pw[g], cb[8 * g : 8 * g + 8].reshape(8 * T, C))
        chosen = chosen.astype(BF16).reshape(X, M, C)
        xs[a, g] = chosen
        ra[a, 0, 4 * g] = chosen[0]
        for d in range(1, X):
            xcopy[a, g, d] = send(
                xs.at[a, g, d], ra.at[a, 0, 4 * g + d], xsem, (a, g, d - 1), ahead[d]
            )

    ycopy = {}

    def ysend(a, g):
        for d in range(1, X):
            xcopy[a, g, d].wait_recv()
        own = ra.at[a, 0, pl.ds(4 * g, 4)]
        for n, (j, dev) in enumerate(((1, up), (3, down), (4, sib))):
            ycopy[a, g, n] = send(own, ra.at[a, j, pl.ds(4 * g, 4)], ysem, (a, g, n), dev)

    def yforward(a, g):
        for n, j, at, dev in ((0, 1, 0, up), (1, 3, 2, down)):
            ycopy[a, g, n].wait_recv()
            half = pl.ds(4 * g + at, 2)
            ycopy[a, g, 3 + n] = send(ra.at[a, j, half], ra.at[a, 2, half], ysem, (a, g, 3 + n), dev)
            whole = pl.ds(4 * g, 4)
            ycopy[a, g, 4 + j] = send(
                ra.at[a, j, whole], ra.at[a, 4 + j, whole], ysem, (a, g, 4 + j), sib
            )

    def yfinish(a, g):
        ycopy[a, g, 3].wait_recv()
        ycopy[a, g, 4].wait_recv()
        whole = pl.ds(4 * g, 4)
        ycopy[a, g, 6] = send(ra.at[a, 2, whole], ra.at[a, 6, whole], ysem, (a, g, 6), sib)

    def yall(a, g):
        for n in (2, 5, 6, 7):
            ycopy[a, g, n].wait_recv()

    def block(ref, a, j, g):
        return ref[a, j, 4 * g : 4 * g + 4].reshape(G, C)

    def first(g):
        for k, a in ((0, 0), (1, 0), (2, 1)):
            for half in range(2):
                js = range(4 * half, 4 * half + 4)
                rows = jnp.concatenate([block(ra, a, j, g) for j in js], axis=1)
                part = mm(rows, jnp.concatenate([w[k, j] for j in js], axis=1), NT)
                pre[k] = part if half == 0 else pre[k] + part

        def gated(i, _):
            at = pl.ds(pl.multiple_of(i * M, 8), M)
            gate_pre, up_pre, hidden_grad = pre[0, at, :], pre[1, at, :], pre[2, at, :]
            sigma = jax.nn.sigmoid(gate_pre)
            active = gate_pre * sigma
            slope = hidden_grad * up_pre * sigma * (1.0 + gate_pre * (1.0 - sigma))
            for k, value in enumerate((active * up_pre, slope, hidden_grad * active)):
                hs[k, 4 * g + i, :, 0:H] = value.astype(BF16)
            return 0

        lax.fori_loop(0, 4, gated, 0)

    rcopy = {}

    def pieces(a, g):
        def one(j, _):
            if a == 0:
                part = mm(hs[0, 4 * g : 4 * g + 4].reshape(G, C)[:, 0:H], w[2, j])
            else:
                part = mm(hs[1, 4 * g : 4 * g + 4].reshape(G, C)[:, 0:H], w[0, j])
                part += mm(hs[2, 4 * g : 4 * g + 4].reshape(G, C)[:, 0:H], w[1, j])
            po[a, g, j] = part.astype(BF16).reshape(X, M, C)
            return 0

        lax.fori_loop(0, 8, one, 0)
        for n in (2, 1, 3, 0):
            rcopy[a, g, n] = send(po.at[a, g, 4 + n], pb.at[a, g, n], rsem, (a, g, n), sib)

    def total(a, g, n):
        rcopy[a, g, n].wait_recv()

        def one(i, _):
            po[a, g, n, i] = (po[a, g, n, i].astype(F32) + pb[a, g, n, i].astype(F32)).astype(BF16)
            return 0

        lax.fori_loop(0, 4, one, 0)

    def reduce_far(a, g):
        total(a, g, 2)
        for n, dev in ((0, down), (1, up)):
            rcopy[a, g, 4 + n] = send(
                po.at[a, g, 2, pl.ds(2 * n, 2)], rl.at[a, g, n], rsem, (a, g, 4 + n), dev
            )

    def reduce_near(a, g):
        for n, j, dev in ((0, 1, down), (1, 3, up)):
            total(a, g, j)
            rcopy[a, g, 4 + n].wait_recv()
            for i in range(2):
                po[a, g, j, 2 * n + i] = (
                    po[a, g, j, 2 * n + i].astype(F32) + rl[a, g, n, i].astype(F32)
                ).astype(BF16)
            rcopy[a, g, 6 + n] = send(po.at[a, g, j], fr.at[a, g, n], rsem, (a, g, 6 + n), dev)

    bcopy = {}

    def give_back(a, g):
        for n in (0, 6, 7):
            rcopy[a, g, n].wait_recv()

        def one(i, _):
            fb[a, g, i] = (
                po[a, g, 0, i].astype(F32)
                + pb[a, g, 0, i].astype(F32)
                + fr[a, g, 0, i].astype(F32)
                + fr[a, g, 1, i].astype(F32)
            ).astype(BF16)
            return 0

        lax.fori_loop(0, 4, one, 0)
        ret[a, g, 0] = fb[a, g, 0]
        for d in range(1, X):
            bcopy[a, g, d] = send(fb.at[a, g, d], ret.at[a, g, d], bsem, (a, g, d - 1), behind[d])

    def combine(a, g):
        for d in range(1, X):
            bcopy[a, g, d].wait_recv()
        rows = ret[a, g].reshape(G, C)
        table = (pw, pu)[a]
        for i in range(8):
            con[a, 8 * g + i] = mm(table[g, :, T * i : T * i + T], rows, TN)

    def gate_terms(g):
        rows = ret[0, g].reshape(G, C)
        dots = jnp.sum(
            xs[1, g].reshape(G, C).astype(F32) * rows.astype(F32), axis=1, keepdims=True
        )
        for i in range(8):
            spread = pu[g, :, T * i : T * i + T].astype(F32) * dots
            ids = rb[8 * g + i, T : T + 16, 0:128].astype(F32)
            gates = rb[8 * g + i, T : T + 16, 128:256].astype(F32)
            parts = jnp.zeros((16, T), F32)
            for d in range(X):
                line = jnp.sum(spread[M * d : M * d + M], axis=0, keepdims=True)
                parts += jnp.where(ids == experts(d), line, 0.0)
            gt[8 * g + i] = parts / gates

    qcopy = {}
    qfirst = {(0, 0): 7, (0, 1): 8, (1, 0): 8, (1, 1): 7}

    def qsend(a, d, s):
        rows = pl.ds(0, T + 16 if a == 0 else T)
        qcopy[a, d, s] = send(
            zr.at[a, d, s, rows], zr.at[a, d, s - 1, rows], qsem, (a, d, s - 1), (right, left)[d]
        )

    def qstart(a):
        for d in range(2):
            s = qfirst[a, d]
            place = (LEFT, RIGHT)[d][s]
            zr[a, d, s, 0:T] = con[a, place].astype(BF16)
            if a == 0:
                zr[a, d, s, T : T + 16, 0:128] = gt[place].astype(BF16)
                zr[a, d, s, T : T + 16, 128:256] = jnp.zeros((16, 128), BF16)
            qsend(a, d, s)

    def qstep(a, back):
        for d in range(2):
            s = qfirst[a, d] - back
            if s < 0:
                continue
            qcopy[a, d, s + 1].wait_recv()
            if s == 0:
                continue
            place = (LEFT, RIGHT)[d][s]
            zr[a, d, s, 0:T] = (zr[a, d, s, 0:T].astype(F32) + con[a, place]).astype(BF16)
            if a == 0:
                zr[a, d, s, T : T + 16, 0:128] = (
                    zr[a, d, s, T : T + 16, 0:128].astype(F32) + gt[place]
                ).astype(BF16)
            qsend(a, d, s)

    sent_local = []

    def turn():
        for k in range(3):
            ht[k] = jnp.transpose(hs[k].reshape(2 * G, C))

    def weight_grads(j):
        col = pl.multiple_of((((y + Y - j % 4) % Y) * 2 + (c + j // 4) % 2) * C, C)
        for k, n, a in ((0, 1, 0), (1, 2, 0), (2, 0, 1)):
            gs[k, j] = mm(ht[n, 0:H, :], ra[a, j].reshape(2 * G, C)).astype(BF16)
            dst = gin.at[k, :, pl.ds(col, C)] if k < 2 else gout.at[:, pl.ds(col, C)]
            sent_local.append(pltpu.make_async_copy(gs.at[k, j], dst, osem.at[k, j]))
            sent_local[-1].start()

    def prepare():
        hs[:, :, :, 128:256] = jnp.zeros((3, 8, M, 128), BF16)

    def loaded():
        for load in loads:
            load.wait()

    gcopy = {}

    def finish(a):
        branch = con[a, 0] + zr[a, 0, 0, 0:T].astype(F32) + zr[a, 1, 0, 0:T].astype(F32)
        if a == 0:
            lines = slice(T, T + 16)
            here = gt[0] + zr[0, 0, 0, lines, 0:128].astype(F32) + zr[0, 1, 0, lines, 0:128].astype(F32)
            gb[0] = here[0:8]
            for r in range(1, 8):
                gcopy[r] = send(gb.at[0], gb.at[r], gsem, (r - 1,), peers[r])
            res[...] = (sh[...].astype(F32) - branch).astype(BF16)
        else:
            car[...] = (fg[...].astype(F32) + branch).astype(BF16)

    def gate_total():
        for r in range(1, 8):
            gcopy[r].wait_recv()
        gat[...] = sum(gb[r] for r in range(8))

    steps = [
        (zstep, 1),
        (prepare,),
        (zstep, 2),
        (zstep, 3),
        (zstep, 4),
        (zstep, 5),
        (slots, 0),
        (xsend, 0, 0),
        (xsend, 1, 0),
        (zstep, 6),
        (ysend, 0, 0),
        (ysend, 1, 0),
        (zstep, 7),
        (yforward, 0, 0),
        (zstep, 8),
        (yforward, 1, 0),
        (loaded,),
        (zstep, 9),
        (slots, 1),
        (xsend, 0, 1),
        (xsend, 1, 1),
        (yfinish, 0, 0),
        (ysend, 0, 1),
        (yfinish, 1, 0),
        (ysend, 1, 1),
        (yall, 0, 0),
        (yall, 1, 0),
        (first, 0),
        (yforward, 0, 1),
        (pieces, 0, 0),
        (yforward, 1, 1),
        (reduce_far, 0, 0),
        (yfinish, 0, 1),
        (pieces, 1, 0),
        (yfinish, 1, 1),
        (reduce_near, 0, 0),
        (yall, 0, 1),
        (reduce_far, 1, 0),
        (yall, 1, 1),
        (first, 1),
        (pieces, 0, 1),
        (reduce_near, 1, 0),
        (reduce_far, 0, 1),
        (give_back, 0, 0),
        (pieces, 1, 1),
        (reduce_near, 0, 1),
        (reduce_far, 1, 1),
        (give_back, 1, 0),
        (turn,),
        (combine, 0, 0),
        (give_back, 0, 1),
        (reduce_near, 1, 1),
        (gate_terms, 0),
        (combine, 0, 1),
        (gate_terms, 1),
        (qstart, 0),
        (combine, 1, 0),
        (give_back, 1, 1),
        (qstep, 0, 1),
        (weight_grads, 0),
        (combine, 1, 1),
        (qstart, 1),
        (qstep, 0, 2),
        (weight_grads, 1),
        (qstep, 1, 1),
        (qstep, 0, 3),
        (weight_grads, 2),
        (qstep, 1, 2),
        (qstep, 0, 4),
        (weight_grads, 3),
        (qstep, 1, 3),
        (qstep, 0, 5),
        (weight_grads, 4),
        (qstep, 1, 4),
        (qstep, 0, 6),
        (weight_grads, 5),
        (qstep, 1, 5),
        (qstep, 0, 7),
        (weight_grads, 6),
        (qstep, 1, 6),
        (qstep, 0, 8),
        (finish, 0),
        (weight_grads, 7),
        (qstep, 1, 7),
        (gate_total,),
        (qstep, 1, 8),
        (finish, 1),
    ]
    for step, *at in steps:
        step(*at)
    for copy in sent:
        copy.wait_send()
    for copy in sent_local:
        copy.wait()


def settle(res, car, gat, gin, gout, res_out, car_out, gat_out, gin_out, gout_out, sem):
    pairs = ((gin, gin_out), (gout, gout_out), (res, res_out), (car, car_out))
    copies = [pltpu.make_async_copy(src, dst, sem.at[n]) for n, (src, dst) in enumerate(pairs)]
    for copy in copies:
        copy.start()
    gat_out[...] = gat[0:6]
    for copy in copies:
        copy.wait()


def body(first_half, second_half, first_grad, second_grad, expert_ids, gate_weights, expert_in, expert_out):
    vmem, hbm = pl.BlockSpec(memory_space=pltpu.VMEM), pl.BlockSpec(memory_space=pl.ANY)
    dma = pltpu.SemaphoreType.DMA
    shape = jax.ShapeDtypeStruct
    res, car, gat, gin, gout = pl.pallas_call(
        kernel,
        out_shape=(
            shape((T, C), BF16),
            shape((T, C), BF16),
            shape((8, T), F32),
            shape((2, H, D), BF16),
            shape((H, D), BF16),
        ),
        in_specs=[vmem] * 6 + [hbm] * 2,
        out_specs=(vmem, vmem, vmem, hbm, hbm),
        scratch_shapes=[
            pltpu.VMEM((16, T + 16, C), BF16),
            pltpu.VMEM((16, T, C), BF16),
            pltpu.VMEM((2, G, 8 * T), BF16),
            pltpu.VMEM((2, G, 8 * T), BF16),
            pltpu.VMEM((2, 2, X, M, C), BF16),
            pltpu.VMEM((2, 8, 8, M, C), BF16),
            pltpu.VMEM((3, 8, H, C), BF16),
            pltpu.VMEM((3, G, H), F32),
            pltpu.VMEM((3, 8, M, C), BF16),
            pltpu.VMEM((3, C, 2 * G), BF16),
            pltpu.VMEM((2, 2, 8, X, M, C), BF16),
            pltpu.VMEM((2, 2, 4, X, M, C), BF16),
            pltpu.VMEM((2, 2, 2, 2, M, C), BF16),
            pltpu.VMEM((2, 2, 2, X, M, C), BF16),
            pltpu.VMEM((2, 2, X, M, C), BF16),
            pltpu.VMEM((2, 2, X, M, C), BF16),
            pltpu.VMEM((2, 16, T, C), F32),
            pltpu.VMEM((16, 16, T), F32),
            pltpu.VMEM((2, 2, 9, T + 16, C), BF16),
            pltpu.VMEM((8, 8, T), F32),
            pltpu.VMEM((3, 8, H, C), BF16),
            dma((2, 2, 16)),
            dma((2, 2, 2, 3)),
            dma((2, 2, 2, 8)),
            dma((2, 2, 2, 8)),
            dma((2, 2, 2, 3)),
            dma((2, 2, 2, 8)),
            dma((2, 7)),
            dma((3, 8)),
            dma((3, 8)),
        ],
        compiler_params=pltpu.CompilerParams(
            collective_id=0, has_side_effects=True, vmem_limit_bytes=58 * 2**20
        ),
    )(first_half, second_grad, second_half, first_grad, expert_ids.T, gate_weights.T, expert_in[0], expert_out[0])
    res, car, gat, gin, gout = pl.pallas_call(
        settle,
        out_shape=(
            shape((T, C), BF16),
            shape((T, C), BF16),
            shape((6, T), F32),
            shape((2, H, D), BF16),
            shape((H, D), BF16),
        ),
        in_specs=[vmem] * 5,
        out_specs=(hbm, hbm, vmem, hbm, hbm),
        scratch_shapes=[dma((4,))],
    )(res, car, gat, gin, gout)
    return res, car, gat.T, gin[None], gout[None]


def solution(mesh):
    tokens = P("expert", "tensor")
    routes = P("expert", None)
    weights = (P("expert", None, "tensor", None), P("expert", "tensor", None))
    return jax.shard_map(
        body,
        mesh=mesh,
        in_specs=(tokens, tokens, tokens, tokens, routes, routes, *weights),
        out_specs=(tokens, tokens, routes, *weights),
        check_vma=False,
    )
```

```python
import jax
import jax.numpy as jnp
from jax import lax
from jax.experimental import pallas as pl
from jax.experimental.pallas import tpu as pltpu
from jax.sharding import PartitionSpec as P

F32, BF16 = jnp.float32, jnp.bfloat16
X, Y, Z = 4, 4, 16
T, C, H, D, CAP, K = 128, 256, 176, 2048, 14, 8
M = 8 * CAP
G = 4 * M
RIGHT = (0, 1, 2, 3, 4, 8, 9, 10, 11)
LEFT = (0, 5, 6, 7, 12, 13, 14, 15, 11)
NT = (((1,), (1,)), ((), ()))
TN = (((0,), (0,)), ((), ()))
MESH = pl.DeviceIdType.MESH


def mm(a, b, dims=(((1,), (0,)), ((), ()))):
    return lax.dot_general(a, b, dims, preferred_element_type=F32)


def kernel(
    fh, sg, sh, fg, ids, gates, win, wdn,
    res, car, gat, gin, gout,
    rb, cb, pu, pw, xs, ra, w, pre, hs, ht, po, pb, rl, fr, fb, ret, con, gt, zr, gb, gs,
    zsem, xsem, ysem, rsem, bsem, qsem, gsem, wsem, osem,
):
    e, t = lax.axis_index("expert"), lax.axis_index("tensor")
    x, z, y, c = e // Z, e % Z, t // 2, t % 2
    right, left = (x * Z + (z + 1) % Z, t), (x * Z + (z + Z - 1) % Z, t)
    up, down = (e, ((y + 1) % Y) * 2 + c), (e, ((y + Y - 1) % Y) * 2 + c)
    sib = (e, y * 2 + 1 - c)
    ahead = [(((x + d) % X) * Z + z, t) for d in range(X)]
    behind = [(((x + X - d) % X) * Z + z, t) for d in range(X)]
    peers = [(e, (t + r) % 8) for r in range(8)]

    loads = []
    for j in range(8):
        col = pl.multiple_of((((y + Y - j % 4) % Y) * 2 + (c + j // 4) % 2) * C, C)
        for k in range(3):
            src = win.at[k, :, pl.ds(col, C)] if k < 2 else wdn.at[:, pl.ds(col, C)]
            loads.append(pltpu.make_async_copy(src, w.at[k, j], wsem.at[k, j]))
            loads[-1].start()
    rb[0, 0:T, :] = fh[...]
    blank = jnp.ones((10, T), F32)
    names = jnp.concatenate([ids[...].astype(F32), -blank], axis=0)
    rb[0, T : T + 16, 0:128] = names.astype(BF16)
    rb[0, T : T + 16, 128:256] = jnp.concatenate([gates[...].astype(F32), blank], axis=0).astype(BF16)
    cb[0] = sg[...]

    barrier = pltpu.get_barrier_semaphore()
    for dev in [right, left, *ahead[1:], *peers[1:]]:
        pl.semaphore_signal(barrier, inc=1, device_id=dev, device_id_type=MESH)
    pl.semaphore_wait(barrier, 12)

    sent = []

    def send(src, dst, sems, at, dev):
        copy = pltpu.make_async_remote_copy(
            src_ref=src,
            dst_ref=dst,
            send_sem=sems.at[(0, *at)],
            recv_sem=sems.at[(1, *at)],
            device_id=dev,
            device_id_type=MESH,
        )
        copy.start()
        sent.append(copy)
        return copy

    zcopy = {}
    zlast = {(0, 0): 8, (0, 1): 7, (1, 0): 7, (1, 1): 8}

    def zstep(s):
        for a in range(2):
            buf = (rb, cb)[a]
            for d in range(2):
                place = (RIGHT, LEFT)[d]
                if s > 1 and s - 1 <= zlast[a, d]:
                    zcopy[a, d, s - 1].wait_recv()
                if s <= zlast[a, d]:
                    zcopy[a, d, s] = send(
                        buf.at[place[s - 1]], buf.at[place[s]], zsem, (a, place[s]), (right, left)[d]
                    )

    before = lax.broadcasted_iota(jnp.int32, (T, T), 0) < lax.broadcasted_iota(jnp.int32, (T, T), 1)
    before = jnp.where(before, 1.0, 0.0).astype(BF16)

    def experts(d):
        return (((x + d) % X) * Z + z).astype(F32)

    def slots(g):
        ids = rb[8 * g : 8 * g + 8, T : T + 16, 0:128].astype(F32)
        gates = rb[8 * g : 8 * g + 8, T : T + 16, 128:256].astype(F32)
        member, weight = [], []
        for d in range(X):
            hit = ids == experts(d)
            member.append(jnp.sum(jnp.where(hit, 1.0, 0.0), axis=1))
            weight.append(jnp.sum(jnp.where(hit, gates, 0.0), axis=1))
        member, weight = jnp.concatenate(member, axis=0), jnp.concatenate(weight, axis=0)
        rank = mm(member.astype(BF16), before)
        source = lax.broadcasted_iota(jnp.int32, (32, T), 0) % 8
        place = jnp.where(member > 0.5, rank + (CAP * source).astype(F32), -1.0)
        row = lax.broadcasted_iota(jnp.int32, (M, T), 0).astype(F32)
        for d in range(X):
            for i in range(8):
                n = 8 * d + i
                here = row == place[n : n + 1, :]
                pu[g, M * d : M * d + M, T * i : T * i + T] = jnp.where(here, 1.0, 0.0).astype(BF16)
                pw[g, M * d : M * d + M, T * i : T * i + T] = jnp.where(
                    here, jnp.broadcast_to(weight[n : n + 1, :], (M, T)), 0.0
                ).astype(BF16)

    xcopy = {}

    def xsend(a, g):
        if a == 0:
            chosen = mm(pu[g], rb[8 * g : 8 * g + 8, 0:T, :].reshape(8 * T, C))
        else:
            chosen = mm(pw[g], cb[8 * g : 8 * g + 8].reshape(8 * T, C))
        chosen = chosen.astype(BF16).reshape(X, M, C)
        xs[a, g] = chosen
        ra[a, 0, 4 * g] = chosen[0]
        for d in range(1, X):
            xcopy[a, g, d] = send(
                xs.at[a, g, d], ra.at[a, 0, 4 * g + d], xsem, (a, g, d - 1), ahead[d]
            )

    ycopy = {}

    def ysend(a, g):
        for d in range(1, X):
            xcopy[a, g, d].wait_recv()
        own = ra.at[a, 0, pl.ds(4 * g, 4)]
        for n, (j, dev) in enumerate(((1, up), (3, down), (4, sib))):
            ycopy[a, g, n] = send(own, ra.at[a, j, pl.ds(4 * g, 4)], ysem, (a, g, n), dev)

    def yforward(a, g):
        for n, j, at, dev in ((0, 1, 0, up), (1, 3, 2, down)):
            ycopy[a, g, n].wait_recv()
            half = pl.ds(4 * g + at, 2)
            ycopy[a, g, 3 + n] = send(ra.at[a, j, half], ra.at[a, 2, half], ysem, (a, g, 3 + n), dev)
            whole = pl.ds(4 * g, 4)
            ycopy[a, g, 4 + j] = send(
                ra.at[a, j, whole], ra.at[a, 4 + j, whole], ysem, (a, g, 4 + j), sib
            )

    def yfinish(a, g):
        ycopy[a, g, 3].wait_recv()
        ycopy[a, g, 4].wait_recv()
        whole = pl.ds(4 * g, 4)
        ycopy[a, g, 6] = send(ra.at[a, 2, whole], ra.at[a, 6, whole], ysem, (a, g, 6), sib)

    def yall(a, g):
        for n in (2, 5, 6, 7):
            ycopy[a, g, n].wait_recv()

    def block(ref, a, j, g):
        return ref[a, j, 4 * g : 4 * g + 4].reshape(G, C)

    def first(g):
        for k, a in ((0, 0), (1, 0), (2, 1)):
            for half in range(2):
                js = range(4 * half, 4 * half + 4)
                rows = jnp.concatenate([block(ra, a, j, g) for j in js], axis=1)
                part = mm(rows, jnp.concatenate([w[k, j] for j in js], axis=1), NT)
                pre[k] = part if half == 0 else pre[k] + part

        def gated(i, _):
            at = pl.ds(pl.multiple_of(i * M, 8), M)
            gate_pre, up_pre, hidden_grad = pre[0, at, :], pre[1, at, :], pre[2, at, :]
            sigma = jax.nn.sigmoid(gate_pre)
            active = gate_pre * sigma
            slope = hidden_grad * up_pre * sigma * (1.0 + gate_pre * (1.0 - sigma))
            for k, value in enumerate((active * up_pre, slope, hidden_grad * active)):
                hs[k, 4 * g + i, :, 0:H] = value.astype(BF16)
            return 0

        lax.fori_loop(0, 4, gated, 0)

    rcopy = {}

    def pieces(a, g):
        def one(j, _):
            if a == 0:
                part = mm(hs[0, 4 * g : 4 * g + 4].reshape(G, C)[:, 0:H], w[2, j])
            else:
                part = mm(hs[1, 4 * g : 4 * g + 4].reshape(G, C)[:, 0:H], w[0, j])
                part += mm(hs[2, 4 * g : 4 * g + 4].reshape(G, C)[:, 0:H], w[1, j])
            po[a, g, j] = part.astype(BF16).reshape(X, M, C)
            return 0

        lax.fori_loop(0, 8, one, 0)
        for n in (2, 1, 3, 0):
            rcopy[a, g, n] = send(po.at[a, g, 4 + n], pb.at[a, g, n], rsem, (a, g, n), sib)

    def total(a, g, n):
        rcopy[a, g, n].wait_recv()

        def one(i, _):
            po[a, g, n, i] = (po[a, g, n, i].astype(F32) + pb[a, g, n, i].astype(F32)).astype(BF16)
            return 0

        lax.fori_loop(0, 4, one, 0)

    def reduce_far(a, g):
        total(a, g, 2)
        for n, dev in ((0, down), (1, up)):
            rcopy[a, g, 4 + n] = send(
                po.at[a, g, 2, pl.ds(2 * n, 2)], rl.at[a, g, n], rsem, (a, g, 4 + n), dev
            )

    def reduce_near(a, g):
        for n, j, dev in ((0, 1, down), (1, 3, up)):
            total(a, g, j)
            rcopy[a, g, 4 + n].wait_recv()
            for i in range(2):
                po[a, g, j, 2 * n + i] = (
                    po[a, g, j, 2 * n + i].astype(F32) + rl[a, g, n, i].astype(F32)
                ).astype(BF16)
            rcopy[a, g, 6 + n] = send(po.at[a, g, j], fr.at[a, g, n], rsem, (a, g, 6 + n), dev)

    bcopy = {}

    def give_back(a, g):
        for n in (0, 6, 7):
            rcopy[a, g, n].wait_recv()

        def one(i, _):
            fb[a, g, i] = (
                po[a, g, 0, i].astype(F32)
                + pb[a, g, 0, i].astype(F32)
                + fr[a, g, 0, i].astype(F32)
                + fr[a, g, 1, i].astype(F32)
            ).astype(BF16)
            return 0

        lax.fori_loop(0, 4, one, 0)
        ret[a, g, 0] = fb[a, g, 0]
        for d in range(1, X):
            bcopy[a, g, d] = send(fb.at[a, g, d], ret.at[a, g, d], bsem, (a, g, d - 1), behind[d])

    def combine(a, g):
        for d in range(1, X):
            bcopy[a, g, d].wait_recv()
        rows = ret[a, g].reshape(G, C)
        table = (pw, pu)[a]
        for i in range(8):
            con[a, 8 * g + i] = mm(table[g, :, T * i : T * i + T], rows, TN)

    def gate_terms(g):
        rows = ret[0, g].reshape(G, C)
        dots = jnp.sum(
            xs[1, g].reshape(G, C).astype(F32) * rows.astype(F32), axis=1, keepdims=True
        )
        for i in range(8):
            spread = pu[g, :, T * i : T * i + T].astype(F32) * dots
            ids = rb[8 * g + i, T : T + 16, 0:128].astype(F32)
            gates = rb[8 * g + i, T : T + 16, 128:256].astype(F32)
            parts = jnp.zeros((16, T), F32)
            for d in range(X):
                line = jnp.sum(spread[M * d : M * d + M], axis=0, keepdims=True)
                parts += jnp.where(ids == experts(d), line, 0.0)
            gt[8 * g + i] = parts / gates

    qcopy = {}
    qfirst = {(0, 0): 7, (0, 1): 8, (1, 0): 8, (1, 1): 7}

    def qsend(a, d, h, s):
        rows = pl.ds(T // 2 * h, T // 2 + (16 if h == 1 and a == 0 else 0))
        qcopy[a, d, h, s] = send(
            zr.at[a, d, s, rows], zr.at[a, d, s - 1, rows], qsem, (a, d, h, s - 1), (right, left)[d]
        )

    def qstart(a):
        for h, d in ((0, 0), (0, 1), (1, 0), (1, 1)):
            s = qfirst[a, d]
            place = (LEFT, RIGHT)[d][s]
            rows = slice(T // 2 * h, T // 2 * h + T // 2)
            zr[a, d, s, rows] = con[a, place, rows].astype(BF16)
            if a == 0 and h == 1:
                zr[a, d, s, T : T + 16, 0:128] = gt[place].astype(BF16)
                zr[a, d, s, T : T + 16, 128:256] = jnp.zeros((16, 128), BF16)
            qsend(a, d, h, s)

    def qstep(a, back):
        for h, d in ((0, 0), (0, 1), (1, 0), (1, 1)):
            s = qfirst[a, d] - back
            if s < 0:
                continue
            qcopy[a, d, h, s + 1].wait_recv()
            if s == 0:
                continue
            place = (LEFT, RIGHT)[d][s]
            rows = slice(T // 2 * h, T // 2 * h + T // 2)
            zr[a, d, s, rows] = (zr[a, d, s, rows].astype(F32) + con[a, place, rows]).astype(BF16)
            if a == 0 and h == 1:
                zr[a, d, s, T : T + 16, 0:128] = (
                    zr[a, d, s, T : T + 16, 0:128].astype(F32) + gt[place]
                ).astype(BF16)
            qsend(a, d, h, s)

    sent_local = []

    def turn():
        for k in range(3):
            ht[k] = jnp.transpose(hs[k].reshape(2 * G, C))

    def weight_grads(j):
        col = pl.multiple_of((((y + Y - j % 4) % Y) * 2 + (c + j // 4) % 2) * C, C)
        for k, n, a in ((0, 1, 0), (1, 2, 0), (2, 0, 1)):
            gs[k, j] = mm(ht[n, 0:H, :], ra[a, j].reshape(2 * G, C)).astype(BF16)
            dst = gin.at[k, :, pl.ds(col, C)] if k < 2 else gout.at[:, pl.ds(col, C)]
            sent_local.append(pltpu.make_async_copy(gs.at[k, j], dst, osem.at[k, j]))
            sent_local[-1].start()

    def prepare():
        hs[:, :, :, 128:256] = jnp.zeros((3, 8, M, 128), BF16)

    def loaded():
        for load in loads:
            load.wait()

    gcopy = {}

    def finish(a):
        branch = con[a, 0] + zr[a, 0, 0, 0:T].astype(F32) + zr[a, 1, 0, 0:T].astype(F32)
        if a == 0:
            lines = slice(T, T + 16)
            here = gt[0] + zr[0, 0, 0, lines, 0:128].astype(F32) + zr[0, 1, 0, lines, 0:128].astype(F32)
            gb[0] = here[0:8]
            for r in range(1, 8):
                gcopy[r] = send(gb.at[0], gb.at[r], gsem, (r - 1,), peers[r])
            res[...] = (sh[...].astype(F32) - branch).astype(BF16)
        else:
            car[...] = (fg[...].astype(F32) + branch).astype(BF16)

    def gate_total():
        for r in range(1, 8):
            gcopy[r].wait_recv()
        gat[...] = sum(gb[r] for r in range(8))

    steps = [
        (zstep, 1),
        (prepare,),
        (zstep, 2),
        (zstep, 3),
        (zstep, 4),
        (zstep, 5),
        (slots, 0),
        (xsend, 0, 0),
        (xsend, 1, 0),
        (zstep, 6),
        (ysend, 0, 0),
        (zstep, 7),
        (ysend, 1, 0),
        (zstep, 8),
        (yforward, 0, 0),
        (loaded,),
        (zstep, 9),
        (yforward, 1, 0),
        (slots, 1),
        (xsend, 0, 1),
        (xsend, 1, 1),
        (yfinish, 0, 0),
        (ysend, 0, 1),
        (yfinish, 1, 0),
        (ysend, 1, 1),
        (yall, 0, 0),
        (yall, 1, 0),
        (first, 0),
        (yforward, 0, 1),
        (pieces, 0, 0),
        (yforward, 1, 1),
        (reduce_far, 0, 0),
        (yfinish, 0, 1),
        (pieces, 1, 0),
        (yfinish, 1, 1),
        (reduce_near, 0, 0),
        (yall, 0, 1),
        (reduce_far, 1, 0),
        (yall, 1, 1),
        (first, 1),
        (pieces, 0, 1),
        (reduce_near, 1, 0),
        (reduce_far, 0, 1),
        (give_back, 0, 0),
        (pieces, 1, 1),
        (reduce_near, 0, 1),
        (reduce_far, 1, 1),
        (give_back, 1, 0),
        (combine, 0, 0),
        (give_back, 0, 1),
        (reduce_near, 1, 1),
        (gate_terms, 0),
        (combine, 0, 1),
        (gate_terms, 1),
        (qstart, 0),
        (combine, 1, 0),
        (give_back, 1, 1),
        (qstep, 0, 1),
        (turn,),
        (combine, 1, 1),
        (qstart, 1),
        (weight_grads, 0),
        (qstep, 0, 2),
        (weight_grads, 1),
        (qstep, 1, 1),
        (qstep, 0, 3),
        (weight_grads, 2),
        (qstep, 1, 2),
        (qstep, 0, 4),
        (weight_grads, 3),
        (qstep, 1, 3),
        (qstep, 0, 5),
        (weight_grads, 4),
        (qstep, 1, 4),
        (qstep, 0, 6),
        (weight_grads, 5),
        (qstep, 1, 5),
        (qstep, 0, 7),
        (weight_grads, 6),
        (qstep, 1, 6),
        (qstep, 0, 8),
        (finish, 0),
        (weight_grads, 7),
        (qstep, 1, 7),
        (gate_total,),
        (qstep, 1, 8),
        (finish, 1),
    ]
    for step, *at in steps:
        step(*at)
    for copy in sent:
        copy.wait_send()
    for copy in sent_local:
        copy.wait()


def settle(res, car, gat, gin, gout, res_out, car_out, gat_out, gin_out, gout_out, sem):
    pairs = ((gin, gin_out), (gout, gout_out), (res, res_out), (car, car_out))
    copies = [pltpu.make_async_copy(src, dst, sem.at[n]) for n, (src, dst) in enumerate(pairs)]
    for copy in copies:
        copy.start()
    gat_out[...] = gat[0:6]
    for copy in copies:
        copy.wait()


def body(first_half, second_half, first_grad, second_grad, expert_ids, gate_weights, expert_in, expert_out):
    vmem, hbm = pl.BlockSpec(memory_space=pltpu.VMEM), pl.BlockSpec(memory_space=pl.ANY)
    dma = pltpu.SemaphoreType.DMA
    shape = jax.ShapeDtypeStruct
    res, car, gat, gin, gout = pl.pallas_call(
        kernel,
        out_shape=(
            shape((T, C), BF16),
            shape((T, C), BF16),
            shape((8, T), F32),
            shape((2, H, D), BF16),
            shape((H, D), BF16),
        ),
        in_specs=[vmem] * 6 + [hbm] * 2,
        out_specs=(vmem, vmem, vmem, hbm, hbm),
        scratch_shapes=[
            pltpu.VMEM((16, T + 16, C), BF16),
            pltpu.VMEM((16, T, C), BF16),
            pltpu.VMEM((2, G, 8 * T), BF16),
            pltpu.VMEM((2, G, 8 * T), BF16),
            pltpu.VMEM((2, 2, X, M, C), BF16),
            pltpu.VMEM((2, 8, 8, M, C), BF16),
            pltpu.VMEM((3, 8, H, C), BF16),
            pltpu.VMEM((3, G, H), F32),
            pltpu.VMEM((3, 8, M, C), BF16),
            pltpu.VMEM((3, C, 2 * G), BF16),
            pltpu.VMEM((2, 2, 8, X, M, C), BF16),
            pltpu.VMEM((2, 2, 4, X, M, C), BF16),
            pltpu.VMEM((2, 2, 2, 2, M, C), BF16),
            pltpu.VMEM((2, 2, 2, X, M, C), BF16),
            pltpu.VMEM((2, 2, X, M, C), BF16),
            pltpu.VMEM((2, 2, X, M, C), BF16),
            pltpu.VMEM((2, 16, T, C), F32),
            pltpu.VMEM((16, 16, T), F32),
            pltpu.VMEM((2, 2, 9, T + 16, C), BF16),
            pltpu.VMEM((8, 8, T), F32),
            pltpu.VMEM((3, 8, H, C), BF16),
            dma((2, 2, 16)),
            dma((2, 2, 2, 3)),
            dma((2, 2, 2, 8)),
            dma((2, 2, 2, 8)),
            dma((2, 2, 2, 3)),
            dma((2, 2, 2, 2, 8)),
            dma((2, 7)),
            dma((3, 8)),
            dma((3, 8)),
        ],
        compiler_params=pltpu.CompilerParams(
            collective_id=0, has_side_effects=True, vmem_limit_bytes=58 * 2**20
        ),
    )(first_half, second_grad, second_half, first_grad, expert_ids.T, gate_weights.T, expert_in[0], expert_out[0])
    res, car, gat, gin, gout = pl.pallas_call(
        settle,
        out_shape=(
            shape((T, C), BF16),
            shape((T, C), BF16),
            shape((6, T), F32),
            shape((2, H, D), BF16),
            shape((H, D), BF16),
        ),
        in_specs=[vmem] * 5,
        out_specs=(hbm, hbm, vmem, hbm, hbm),
        scratch_shapes=[dma((4,))],
    )(res, car, gat, gin, gout)
    return res, car, gat.T, gin[None], gout[None]


def solution(mesh):
    tokens = P("expert", "tensor")
    routes = P("expert", None)
    weights = (P("expert", None, "tensor", None), P("expert", "tensor", None))
    return jax.shard_map(
        body,
        mesh=mesh,
        in_specs=(tokens, tokens, tokens, tokens, routes, routes, *weights),
        out_specs=(tokens, tokens, routes, *weights),
        check_vma=False,
    )
```
